32 devices in a mesh: seq: 16 (over z, x, core), head: 2 (over y).
Axes of the slice: x: 2, y: 2, z: 4, core: 2. Of those that a mesh axis runs over, the one named last changes fastest.
Arguments:
- queries: bfloat16 [6, 16, 128, 3072], P(None, None, 'seq', 'head'), may hold values from -6 to 6
- key_field: bfloat16 [6, 16, 128, 3072], P(None, None, 'seq', 'head'), may hold values from -6 to 6
- value_field: bfloat16 [6, 16, 128, 3072], P(None, None, 'seq', 'head'), may hold values from -6 to 6
Outputs:
- attended: bfloat16 [6, 16, 128, 3072], P(None, 'head', 'seq')
The draws below stay inside these ranges and needn't reach their ends.
All inputs are finite; a program needn't handle non-finite values.
Results may differ from the reference program's by a relative error of at most 0.0047.
Values may be sent and summed in bfloat16 or wider, within the bound.
A program may use at most 256 MiB of HBM per device.

```python
import jax
import jax.numpy as jnp
from jax import lax

HEADS = 24
HD = 128
TF = 6
TH = 8
TW = 8
HTILES = 2
FTILES = 1
FRAMES = 6
HEIGHT = 16
WIDTH = 128


def rough_field(key):
    shape = (FTILES, TF, HTILES, TH, WIDTH // TW, TW, HEADS * HD)
    return jax.random.truncated_normal(key, -6.0, 6.0, shape, jnp.float32)


def draw_queries(key, part):
    key = jax.random.fold_in(key, 1)
    field = rough_field(key)
    return field.reshape(FRAMES, HEIGHT, WIDTH, HEADS * HD).astype(jnp.bfloat16)


def draw_key_field(key, part):
    key = jax.random.fold_in(key, 2)
    field = rough_field(key)
    return field.reshape(FRAMES, HEIGHT, WIDTH, HEADS * HD).astype(jnp.bfloat16)


def steps_of(key, dims, split, low, largest):
    gain = 1.0
    for axis_at, parts in split:
        steps = jax.random.uniform(jax.random.fold_in(jax.random.fold_in(key, 6), axis_at), (parts,), jnp.float32, low / len(split), largest / len(split))
        gain = gain * jnp.repeat(jnp.exp(steps), dims[axis_at] // parts).reshape((-1,) + (1,) * (len(dims) - 1 - axis_at))
    return gain


def scatter_about(stream_key, extent, scale, bound, pieces=(), held_as=jnp.bfloat16):
    drawn = jax.random.normal(stream_key, extent, jnp.float32) * scale
    if len(pieces) > 0:
        drawn = steps_of(stream_key, extent, pieces, -0.22, 0.18) * drawn
    return jnp.clip(drawn, min=-bound, max=bound).astype(held_as)


def setup_inputs(seed: int = 0) -> dict:
    streams_of = jax.random.split(jax.random.key(seed), 4)
    queries = draw_queries(jax.random.fold_in(streams_of[3], 71), 0)
    key_field = draw_key_field(jax.random.fold_in(streams_of[3], 71), 0)
    value_field = scatter_about(streams_of[2], (FRAMES, HEIGHT, WIDTH, HEADS * HD), 1.0, 6.0, ((2, 16), (3, 2)))
    return {"queries": queries, "key_field": key_field, "value_field": value_field}


def attend_tile(query_rows, key_rows, value_rows, allowed):
    head_count = query_rows.shape[1] // HD
    query_heads = query_rows.reshape(query_rows.shape[0], head_count, HD).astype(jnp.float32)
    key_heads = key_rows.reshape(key_rows.shape[0], head_count, HD).astype(jnp.float32)
    value_heads = value_rows.reshape(value_rows.shape[0], head_count, HD).astype(jnp.float32)
    scores = jnp.einsum("qhd,khd->hqk", query_heads, key_heads) * (HD ** -0.5)
    scores = jnp.where(allowed[None, None, :], scores, -jnp.inf)
    row_max = jnp.max(scores, axis=2, keepdims=True)
    weights = jnp.exp(scores - row_max)
    weight_sum = jnp.sum(weights, axis=2, keepdims=True)
    probabilities = lax.optimization_barrier(weights.astype(jnp.bfloat16))
    combined = jnp.einsum("hqk,khd->qhd", probabilities.astype(jnp.float32), value_heads)
    combined = combined / jnp.transpose(weight_sum, (1, 0, 2))
    return combined.reshape(query_rows.shape[0], -1).astype(jnp.bfloat16)


def reference(queries, key_field, value_field):
    frame_count, row_count, col_count, feat_count = queries.shape
    column_tiles = col_count // TW
    frame_tiles = frame_count // TF
    row_tiles = row_count // TH
    padding = ((0, 0), (0, 0), (TW, TW), (0, 0))
    key_padded = jnp.pad(key_field, padding)
    value_padded = jnp.pad(value_field, padding)

    def one_column(column):
        offset = (column * TW).astype(jnp.int32)
        key_column = lax.dynamic_slice_in_dim(key_padded, offset, 3 * TW, 2)
        value_column = lax.dynamic_slice_in_dim(value_padded, offset, 3 * TW, 2)
        query_column = lax.dynamic_slice_in_dim(queries, offset, TW, 2)
        col_pos = offset - TW + jnp.arange(3 * TW, dtype=jnp.int32)
        col_ok = (col_pos >= 0) & (col_pos < col_count)
        frame_pieces = []
        for frame_tile in range(frame_tiles):
            f_low = max(0, frame_tile - 1) * TF
            f_high = min(frame_tiles, frame_tile + 2) * TF
            row_pieces = []
            for row_tile in range(row_tiles):
                h_low = max(0, row_tile - 1) * TH
                h_high = min(row_tiles, row_tile + 2) * TH
                allowed = jnp.broadcast_to(col_ok[None, None, :], (f_high - f_low, h_high - h_low, 3 * TW)).reshape(-1)
                key_rows = key_column[f_low:f_high, h_low:h_high].reshape(-1, feat_count)
                value_rows = value_column[f_low:f_high, h_low:h_high].reshape(-1, feat_count)
                query_rows = query_column[frame_tile * TF:(frame_tile + 1) * TF, row_tile * TH:(row_tile + 1) * TH].reshape(-1, feat_count)
                result = attend_tile(query_rows, key_rows, value_rows, allowed)
                row_pieces.append(result.reshape(TF, TH, TW, feat_count))
            frame_pieces.append(jnp.concatenate(row_pieces, 1))
        return jnp.concatenate(frame_pieces, 0)

    columns = lax.map(one_column, jnp.arange(column_tiles, dtype=jnp.int32))
    return jnp.transpose(columns, (1, 2, 0, 3, 4)).reshape(frame_count, row_count, col_count, feat_count)
```

```python
import functools

import jax
import jax.numpy as jnp
from jax import lax
from jax.experimental import pallas as pl
from jax.experimental.pallas import tpu as pltpu
from jax.sharding import PartitionSpec as P

HD = 128
AHEAD = 3
MISSING = 1e30
LOG2E = 1.4426950408889634


def kernel(q_ref, k_ref, v_ref, out_ref, q_buf, kv_buf, o_buf,
           load_sem, send_sem, recv_sem, own_sem, osend_sem, orecv_sem, *, seq, head):
    heads = q_buf.shape[0]
    tokens = q_buf.shape[1]
    frames = o_buf.shape[1]
    rows = out_ref.shape[1]
    me = lax.axis_index("seq")
    part = lax.axis_index("head")
    has_left = me > 0
    has_right = me < seq - 1

    def columns(j):
        return pl.ds(pl.multiple_of(j * HD, HD), HD)

    def loads(h):
        return (
            pltpu.make_async_copy(k_ref.at[:, columns(h)], kv_buf.at[1, h, 0], load_sem.at[0, h]),
            pltpu.make_async_copy(v_ref.at[:, columns(h)], kv_buf.at[1, h, 1], load_sem.at[1, h]),
            pltpu.make_async_copy(q_ref.at[:, columns(h)], q_buf.at[h], load_sem.at[2, h]),
        )

    def to_side(h, side):
        target = me + 1 if side == 0 else me - 1
        return pltpu.make_async_remote_copy(
            src_ref=kv_buf.at[1, h],
            dst_ref=kv_buf.at[0 if side == 0 else 2, h],
            send_sem=send_sem.at[side, h],
            recv_sem=recv_sem.at[side, h],
            device_id={"seq": target},
            device_id_type=pl.DeviceIdType.MESH,
        )

    def out_slices(h, p, sender):
        src = o_buf.at[h, :, pl.ds(pl.multiple_of(p * rows, 16), rows), :]
        dst = out_ref.at[:, :, columns(sender * heads + h)]
        return src, dst

    def to_part(h, step):
        p = lax.rem(part + step, head)
        src, dst = out_slices(h, p, part)
        return pltpu.make_async_remote_copy(
            src_ref=src,
            dst_ref=dst,
            send_sem=osend_sem.at[step, h],
            recv_sem=orecv_sem.at[step, h],
            device_id={"head": p},
            device_id_type=pl.DeviceIdType.MESH,
        )

    def to_self(h):
        src, dst = out_slices(h, part, part)
        return pltpu.make_async_copy(src, dst, own_sem.at[h])

    def start_loads(h, carry):
        for copy in loads(h):
            copy.start()
        return carry

    lax.fori_loop(0, heads, start_loads, 0)

    barrier = pltpu.get_barrier_semaphore()
    for near in (lax.rem(me + 1, seq), lax.rem(me + seq - 1, seq)):
        pl.semaphore_signal(barrier, inc=1, device_id={"seq": near}, device_id_type=pl.DeviceIdType.MESH)
    for step in range(1, head):
        pl.semaphore_signal(barrier, inc=1, device_id={"head": lax.rem(part + step, head)},
                            device_id_type=pl.DeviceIdType.MESH)
    pl.semaphore_wait(barrier, 2 + head - 1)

    def send(h):
        for copy in loads(h):
            copy.wait()

        @pl.when(has_right)
        def _():
            to_side(h, 0).start()

        @pl.when(has_left)
        def _():
            to_side(h, 1).start()

    ahead = min(AHEAD, heads)

    def first_sends(h, carry):
        send(h)
        return carry

    lax.fori_loop(0, ahead, first_sends, 0)

    @pl.when(jnp.logical_not(has_left))
    def _():
        kv_buf[0] = jnp.zeros_like(kv_buf[0])

    @pl.when(jnp.logical_not(has_right))
    def _():
        kv_buf[2] = jnp.zeros_like(kv_buf[2])

    shift = (
        jnp.where(has_left, 0.0, MISSING).astype(jnp.float32),
        jnp.float32(0.0),
        jnp.where(has_right, 0.0, MISSING).astype(jnp.float32),
    )
    chunk = 256 if tokens % 256 == 0 else tokens
    factor = HD ** -0.5 * LOG2E
    per_frame = tokens // frames

    def attend(h):
        def rows_of(c, carry):
            at = pl.ds(pl.multiple_of(c * chunk, chunk), chunk)
            q = q_buf[h, at, :]
            scores = [
                lax.dot_general(q, kv_buf[b, h, 0], (((1,), (1,)), ((), ())),
                                preferred_element_type=jnp.float32)
                for b in range(3)
            ]
            tops = [jnp.max(s, axis=1, keepdims=True) - shift[b] for b, s in enumerate(scores)]
            top = jnp.maximum(jnp.maximum(tops[0], tops[1]), tops[2])
            total = 0.0
            weight_sum = 0.0
            for b in range(3):
                w = jnp.exp2(scores[b] * factor - (top + shift[b]) * factor)
                weight_sum = weight_sum + jnp.sum(w, axis=1, keepdims=True)
                total = total + jnp.dot(w.astype(jnp.bfloat16), kv_buf[b, h, 1],
                                        preferred_element_type=jnp.float32)
            result = (total / weight_sum).astype(jnp.bfloat16)
            o_buf[h, pl.ds(c * (chunk // per_frame), chunk // per_frame)] = result.reshape(
                chunk // per_frame, per_frame, HD)
            return carry

        lax.fori_loop(0, tokens // chunk, rows_of, 0)

    def step_of(h, carry):
        @pl.when(h + ahead < heads)
        def _():
            send(h + ahead)

        @pl.when(has_left)
        def _():
            to_side(h, 0).wait_recv()

        @pl.when(has_right)
        def _():
            to_side(h, 1).wait_recv()

        attend(h)
        to_self(h).start()
        for step in range(1, head):
            to_part(h, step).start()
        return carry

    lax.fori_loop(0, heads, step_of, 0)

    def finish(h, carry):
        @pl.when(has_right)
        def _():
            to_side(h, 0).wait_send()

        @pl.when(has_left)
        def _():
            to_side(h, 1).wait_send()

        to_self(h).wait()
        for step in range(1, head):
            to_part(h, step).wait_send()
            to_part(h, step).wait_recv()
        return carry

    lax.fori_loop(0, heads, finish, 0)


def on_device(queries, key_field, value_field):
    frames, height, width, feat = queries.shape
    seq = lax.axis_size("seq")
    head = lax.axis_size("head")
    heads = feat // HD
    tokens = frames * height * width
    rows = height // head * width
    result = pl.pallas_call(
        functools.partial(kernel, seq=seq, head=head),
        out_shape=jax.ShapeDtypeStruct((frames, rows, feat * head), jnp.bfloat16),
        in_specs=[pl.BlockSpec(memory_space=pl.ANY)] * 3,
        out_specs=pl.BlockSpec(memory_space=pl.ANY),
        scratch_shapes=[
            pltpu.VMEM((heads, tokens, HD), jnp.bfloat16),
            pltpu.VMEM((3, heads, 2, tokens, HD), jnp.bfloat16),
            pltpu.VMEM((heads, frames, height * width, HD), jnp.bfloat16),
            pltpu.SemaphoreType.DMA((3, heads)),
            pltpu.SemaphoreType.DMA((2, heads)),
            pltpu.SemaphoreType.DMA((2, heads)),
            pltpu.SemaphoreType.DMA((heads,)),
            pltpu.SemaphoreType.DMA((head, heads)),
            pltpu.SemaphoreType.DMA((head, heads)),
        ],
        compiler_params=pltpu.CompilerParams(
            collective_id=0, has_side_effects=True, vmem_limit_bytes=56 * 2 ** 20
        ),
        cost_estimate=pl.CostEstimate(
            flops=12 * heads * tokens * tokens * HD,
            bytes_accessed=8 * tokens * feat,
            transcendentals=3 * heads * tokens * tokens,
        ),
        name="tile_attention",
    )(
        queries.reshape(tokens, feat),
        key_field.reshape(tokens, feat),
        value_field.reshape(tokens, feat),
    )
    return result.reshape(frames, height // head, width, feat * head)


def solution(mesh):
    spec = P(None, None, "seq", "head")
    return jax.shard_map(
        on_device, mesh=mesh, in_specs=(spec, spec, spec),
        out_specs=P(None, "head", "seq", None), check_vma=False,
    )
```

```python
import functools

import jax
import jax.numpy as jnp
from jax import lax
from jax.experimental import pallas as pl
from jax.experimental.pallas import tpu as pltpu
from jax.sharding import PartitionSpec as P

HD = 128
AHEAD = 4
RELAY_AHEAD = 2
MISSING = 1e30
LOG2E = 1.4426950408889634


def kernel(q_ref, k_ref, v_ref, out_ref, q_buf, kv_buf, o_buf,
           load_sem, send_sem, recv_sem, own_sem, osend_sem, orecv_sem, *relay_refs, seq, head):
    heads = q_buf.shape[0]
    tokens = q_buf.shape[1]
    frames = o_buf.shape[1]
    rows = out_ref.shape[1]
    me = lax.axis_index("seq")
    part = lax.axis_index("head")
    has_left = me > 0
    has_right = me < seq - 1
    layers = seq // 4
    layer = me // 4
    low = me % 4 == 0
    high = me % 4 == 3
    if relay_refs:
        relay_buf, relay_send, relay_recv = relay_refs

    def columns(j):
        return pl.ds(pl.multiple_of(j * HD, HD), HD)

    def loads(h):
        return (
            pltpu.make_async_copy(k_ref.at[:, columns(h)], kv_buf.at[1, h, 0], load_sem.at[0, h]),
            pltpu.make_async_copy(v_ref.at[:, columns(h)], kv_buf.at[1, h, 1], load_sem.at[1, h]),
            pltpu.make_async_copy(q_ref.at[:, columns(h)], q_buf.at[h], load_sem.at[2, h]),
        )

    def to_side(h, side):
        target = me + 1 if side == 0 else me - 1
        return pltpu.make_async_remote_copy(
            src_ref=kv_buf.at[1, h],
            dst_ref=kv_buf.at[0 if side == 0 else 2, h],
            send_sem=send_sem.at[side, h],
            recv_sem=recv_sem.at[side, h],
            device_id={"seq": target},
            device_id_type=pl.DeviceIdType.MESH,
        )

    def to_relay(h, side):
        return pltpu.make_async_remote_copy(
            src_ref=kv_buf.at[1, h],
            dst_ref=relay_buf.at[h],
            send_sem=send_sem.at[side, h],
            recv_sem=relay_recv.at[h],
            device_id={"seq": me + 4 if side == 0 else me - 4},
            device_id_type=pl.DeviceIdType.MESH,
        )

    def from_relay(h, side):
        return pltpu.make_async_remote_copy(
            src_ref=relay_buf.at[h],
            dst_ref=kv_buf.at[0 if side == 0 else 2, h],
            send_sem=relay_send.at[h],
            recv_sem=recv_sem.at[side, h],
            device_id={"seq": me - 3 if side == 0 else me + 3},
            device_id_type=pl.DeviceIdType.MESH,
        )

    def relayed(h, side, at):
        return h % layers < (at + 1 if side == 0 else layers - at)

    def relays(h, side):
        if side == 0:
            return high & (layer > 0) & relayed(h, 0, layer - 1)
        return low & (layer < layers - 1) & relayed(h, 1, layer + 1)

    def forward(h):
        for side in range(2):
            @pl.when(relays(h, side))
            def _():
                to_relay(h, side).wait_recv()
                from_relay(h, side).start()

    def out_slices(h, p, sender):
        src = o_buf.at[h, :, pl.ds(pl.multiple_of(p * rows, 16), rows), :]
        dst = out_ref.at[:, :, columns(sender * heads + h)]
        return src, dst

    def to_part(h, step):
        p = lax.rem(part + step, head)
        src, dst = out_slices(h, p, part)
        return pltpu.make_async_remote_copy(
            src_ref=src,
            dst_ref=dst,
            send_sem=osend_sem.at[step, h],
            recv_sem=orecv_sem.at[step, h],
            device_id={"head": p},
            device_id_type=pl.DeviceIdType.MESH,
        )

    def to_self(h):
        src, dst = out_slices(h, part, part)
        return pltpu.make_async_copy(src, dst, own_sem.at[h])

    def start_loads(h, carry):
        for copy in loads(h):
            copy.start()
        return carry

    lax.fori_loop(0, heads, start_loads, 0)

    barrier = pltpu.get_barrier_semaphore()
    offsets = (1, seq - 1) + ((3, 4, seq - 3, seq - 4) if relay_refs else ())
    for offset in offsets:
        near = lax.rem(me + offset, seq)
        pl.semaphore_signal(barrier, inc=1, device_id={"seq": near}, device_id_type=pl.DeviceIdType.MESH)
    for step in range(1, head):
        pl.semaphore_signal(barrier, inc=1, device_id={"head": lax.rem(part + step, head)},
                            device_id_type=pl.DeviceIdType.MESH)
    pl.semaphore_wait(barrier, len(offsets) + head - 1)

    def send(h):
        for copy in loads(h):
            copy.wait()

        for side, exists, edge in ((0, has_right, high), (1, has_left, low)):
            if relay_refs:
                by_relay = edge & relayed(h, side, layer)

                @pl.when(exists & by_relay)
                def _():
                    to_relay(h, side).start()

                exists = exists & jnp.logical_not(by_relay)

            @pl.when(exists)
            def _():
                to_side(h, side).start()

    ahead = min(AHEAD, heads)

    def first_sends(h, carry):
        send(h)
        return carry

    lax.fori_loop(0, ahead, first_sends, 0)

    @pl.when(jnp.logical_not(has_left))
    def _():
        kv_buf[0] = jnp.zeros_like(kv_buf[0])

    @pl.when(jnp.logical_not(has_right))
    def _():
        kv_buf[2] = jnp.zeros_like(kv_buf[2])

    shift = (
        jnp.where(has_left, 0.0, MISSING).astype(jnp.float32),
        jnp.float32(0.0),
        jnp.where(has_right, 0.0, MISSING).astype(jnp.float32),
    )
    chunk = 256 if tokens % 256 == 0 else tokens
    factor = HD ** -0.5 * LOG2E
    per_frame = tokens // frames

    relay_ahead = min(RELAY_AHEAD, heads)
    if relay_refs:
        def first_forwards(h, carry):
            forward(h)
            return carry

        lax.fori_loop(0, relay_ahead, first_forwards, 0)

    def attend(h):
        def rows_of(c, carry):
            at = pl.ds(pl.multiple_of(c * chunk, chunk), chunk)
            q = q_buf[h, at, :]
            scores = [
                lax.dot_general(q, kv_buf[b, h, 0], (((1,), (1,)), ((), ())),
                                preferred_element_type=jnp.float32)
                for b in range(3)
            ]
            tops = [jnp.max(s, axis=1, keepdims=True) - shift[b] for b, s in enumerate(scores)]
            top = jnp.maximum(jnp.maximum(tops[0], tops[1]), tops[2])
            total = 0.0
            weight_sum = 0.0
            for b in range(3):
                w = jnp.exp2(scores[b] * factor - (top + shift[b]) * factor)
                weight_sum = weight_sum + jnp.sum(w, axis=1, keepdims=True)
                total = total + jnp.dot(w.astype(jnp.bfloat16), kv_buf[b, h, 1],
                                        preferred_element_type=jnp.float32)
            result = (total / weight_sum).astype(jnp.bfloat16)
            o_buf[h, pl.ds(c * (chunk // per_frame), chunk // per_frame)] = result.reshape(
                chunk // per_frame, per_frame, HD)
            return carry

        lax.fori_loop(0, tokens // chunk, rows_of, 0)

    def step_of(h, carry):
        @pl.when(h + ahead < heads)
        def _():
            send(h + ahead)

        if relay_refs:
            @pl.when(h + relay_ahead < heads)
            def _():
                forward(h + relay_ahead)

        @pl.when(has_left)
        def _():
            to_side(h, 0).wait_recv()

        @pl.when(has_right)
        def _():
            to_side(h, 1).wait_recv()

        attend(h)
        to_self(h).start()
        for step in range(1, head):
            to_part(h, step).start()
        return carry

    lax.fori_loop(0, heads, step_of, 0)

    def finish(h, carry):
        @pl.when(has_right)
        def _():
            to_side(h, 0).wait_send()

        @pl.when(has_left)
        def _():
            to_side(h, 1).wait_send()

        if relay_refs:
            for side in range(2):
                @pl.when(relays(h, side))
                def _():
                    from_relay(h, side).wait_send()

        to_self(h).wait()
        for step in range(1, head):
            to_part(h, step).wait_send()
            to_part(h, step).wait_recv()
        return carry

    lax.fori_loop(0, heads, finish, 0)


def on_device(queries, key_field, value_field):
    frames, height, width, feat = queries.shape
    seq = lax.axis_size("seq")
    head = lax.axis_size("head")
    heads = feat // HD
    tokens = frames * height * width
    rows = height // head * width
    relay_scratch = []
    if seq == 16 and head == 2:
        relay_scratch = [
            pltpu.VMEM((heads, 2, tokens, HD), jnp.bfloat16),
            pltpu.SemaphoreType.DMA((heads,)),
            pltpu.SemaphoreType.DMA((heads,)),
        ]
    result = pl.pallas_call(
        functools.partial(kernel, seq=seq, head=head),
        out_shape=jax.ShapeDtypeStruct((frames, rows, feat * head), jnp.bfloat16),
        in_specs=[pl.BlockSpec(memory_space=pl.ANY)] * 3,
        out_specs=pl.BlockSpec(memory_space=pl.ANY),
        scratch_shapes=[
            pltpu.VMEM((heads, tokens, HD), jnp.bfloat16),
            pltpu.VMEM((3, heads, 2, tokens, HD), jnp.bfloat16),
            pltpu.VMEM((heads, frames, height * width, HD), jnp.bfloat16),
            pltpu.SemaphoreType.DMA((3, heads)),
            pltpu.SemaphoreType.DMA((2, heads)),
            pltpu.SemaphoreType.DMA((2, heads)),
            pltpu.SemaphoreType.DMA((heads,)),
            pltpu.SemaphoreType.DMA((head, heads)),
            pltpu.SemaphoreType.DMA((head, heads)),
        ] + relay_scratch,
        compiler_params=pltpu.CompilerParams(
            collective_id=0, has_side_effects=True, vmem_limit_bytes=56 * 2 ** 20
        ),
        cost_estimate=pl.CostEstimate(
            flops=12 * heads * tokens * tokens * HD,
            bytes_accessed=8 * tokens * feat,
            transcendentals=3 * heads * tokens * tokens,
        ),
        name="tile_attention",
    )(
        queries.reshape(tokens, feat),
        key_field.reshape(tokens, feat),
        value_field.reshape(tokens, feat),
    )
    return result.reshape(frames, height // head, width, feat * head)


def solution(mesh):
    spec = P(None, None, "seq", "head")
    return jax.shard_map(
        on_device, mesh=mesh, in_specs=(spec, spec, spec),
        out_specs=P(None, "head", "seq", None), check_vma=False,
    )
```

```python
import functools

import jax
import jax.numpy as jnp
from jax import lax
from jax.experimental import pallas as pl
from jax.experimental.pallas import tpu as pltpu
from jax.sharding import PartitionSpec as P

HD = 128
AHEAD = 4
RELAY_AHEAD = 2
MISSING = 1e30
LOG2E = 1.4426950408889634


def kernel(q_ref, k_ref, v_ref, out_ref, q_buf, kv_buf, o_buf,
           load_sem, send_sem, recv_sem, own_sem, osend_sem, orecv_sem, *relay_refs, seq, head):
    heads = q_buf.shape[0]
    tokens = q_buf.shape[1]
    frames = o_buf.shape[1]
    rows = out_ref.shape[1]
    me = lax.axis_index("seq")
    part = lax.axis_index("head")
    has_left = me > 0
    has_right = me < seq - 1
    layers = seq // 4
    layer = me // 4
    low = me % 4 == 0
    high = me % 4 == 3
    if relay_refs:
        relay_buf, relay_send, relay_recv = relay_refs

    def columns(j):
        return pl.ds(pl.multiple_of(j * HD, HD), HD)

    def loads(h):
        return (
            pltpu.make_async_copy(k_ref.at[:, columns(h)], kv_buf.at[1, h, 0], load_sem.at[0, h]),
            pltpu.make_async_copy(v_ref.at[:, columns(h)], kv_buf.at[1, h, 1], load_sem.at[1, h]),
            pltpu.make_async_copy(q_ref.at[:, columns(h)], q_buf.at[h], load_sem.at[2, h]),
        )

    def to_side(h, side):
        target = me + 1 if side == 0 else me - 1
        return pltpu.make_async_remote_copy(
            src_ref=kv_buf.at[1, h],
            dst_ref=kv_buf.at[0 if side == 0 else 2, h],
            send_sem=send_sem.at[side, h],
            recv_sem=recv_sem.at[side, h],
            device_id={"seq": target},
            device_id_type=pl.DeviceIdType.MESH,
        )

    def to_relay(h, side):
        return pltpu.make_async_remote_copy(
            src_ref=kv_buf.at[1, h],
            dst_ref=relay_buf.at[h],
            send_sem=send_sem.at[side, h],
            recv_sem=relay_recv.at[h],
            device_id={"seq": me - 2 if side == 0 else me + 2},
            device_id_type=pl.DeviceIdType.MESH,
        )

    def from_relay(h, side):
        return pltpu.make_async_remote_copy(
            src_ref=relay_buf.at[h],
            dst_ref=kv_buf.at[0 if side == 0 else 2, h],
            send_sem=relay_send.at[h],
            recv_sem=recv_sem.at[side, h],
            device_id={"seq": me + 3 if side == 0 else me - 3},
            device_id_type=pl.DeviceIdType.MESH,
        )

    def relayed(h, side, at):
        return h % layers < (layers - 1 - at if side == 0 else at)

    def relays(h, side):
        if side == 0:
            return (me % 4 == 1) & (layer < layers - 1) & relayed(h, 0, layer)
        return (me % 4 == 2) & (layer > 0) & relayed(h, 1, layer)

    def forward(h):
        for side in range(2):
            @pl.when(relays(h, side))
            def _():
                to_relay(h, side).wait_recv()
                from_relay(h, side).start()

    def out_slices(h, p, sender):
        src = o_buf.at[h, :, pl.ds(pl.multiple_of(p * rows, 16), rows), :]
        dst = out_ref.at[:, :, columns(sender * heads + h)]
        return src, dst

    def to_part(h, step):
        p = lax.rem(part + step, head)
        src, dst = out_slices(h, p, part)
        return pltpu.make_async_remote_copy(
            src_ref=src,
            dst_ref=dst,
            send_sem=osend_sem.at[step, h],
            recv_sem=orecv_sem.at[step, h],
            device_id={"head": p},
            device_id_type=pl.DeviceIdType.MESH,
        )

    def to_self(h):
        src, dst = out_slices(h, part, part)
        return pltpu.make_async_copy(src, dst, own_sem.at[h])

    def start_loads(h, carry):
        for copy in loads(h):
            copy.start()
        return carry

    lax.fori_loop(0, heads, start_loads, 0)

    barrier = pltpu.get_barrier_semaphore()
    offsets = (1, seq - 1) + ((2, 3, seq - 2, seq - 3) if relay_refs else ())
    for offset in offsets:
        near = lax.rem(me + offset, seq)
        pl.semaphore_signal(barrier, inc=1, device_id={"seq": near}, device_id_type=pl.DeviceIdType.MESH)
    for step in range(1, head):
        pl.semaphore_signal(barrier, inc=1, device_id={"head": lax.rem(part + step, head)},
                            device_id_type=pl.DeviceIdType.MESH)
    pl.semaphore_wait(barrier, len(offsets) + head - 1)

    def send(h):
        for copy in loads(h):
            copy.wait()

        for side, exists, edge in ((0, has_right, high), (1, has_left, low)):
            if relay_refs:
                by_relay = edge & relayed(h, side, layer)

                @pl.when(exists & by_relay)
                def _():
                    to_relay(h, side).start()

                exists = exists & jnp.logical_not(by_relay)

            @pl.when(exists)
            def _():
                to_side(h, side).start()

    ahead = min(AHEAD, heads)

    def first_sends(h, carry):
        send(h)
        return carry

    lax.fori_loop(0, ahead, first_sends, 0)

    @pl.when(jnp.logical_not(has_left))
    def _():
        kv_buf[0] = jnp.zeros_like(kv_buf[0])

    @pl.when(jnp.logical_not(has_right))
    def _():
        kv_buf[2] = jnp.zeros_like(kv_buf[2])

    shift = (
        jnp.where(has_left, 0.0, MISSING).astype(jnp.float32),
        jnp.float32(0.0),
        jnp.where(has_right, 0.0, MISSING).astype(jnp.float32),
    )
    chunk = 256 if tokens % 256 == 0 else tokens
    factor = HD ** -0.5 * LOG2E
    per_frame = tokens // frames

    relay_ahead = min(RELAY_AHEAD, heads)
    if relay_refs:
        def first_forwards(h, carry):
            forward(h)
            return carry

        lax.fori_loop(0, relay_ahead, first_forwards, 0)

    def attend(h):
        def rows_of(c, carry):
            at = pl.ds(pl.multiple_of(c * chunk, chunk), chunk)
            q = q_buf[h, at, :]
            scores = [
                lax.dot_general(q, kv_buf[b, h, 0], (((1,), (1,)), ((), ())),
                                preferred_element_type=jnp.float32)
                for b in range(3)
            ]
            tops = [jnp.max(s, axis=1, keepdims=True) - shift[b] for b, s in enumerate(scores)]
            top = jnp.maximum(jnp.maximum(tops[0], tops[1]), tops[2])
            total = 0.0
            weight_sum = 0.0
            for b in range(3):
                w = jnp.exp2(scores[b] * factor - (top + shift[b]) * factor)
                weight_sum = weight_sum + jnp.sum(w, axis=1, keepdims=True)
                total = total + jnp.dot(w.astype(jnp.bfloat16), kv_buf[b, h, 1],
                                        preferred_element_type=jnp.float32)
            result = (total / weight_sum).astype(jnp.bfloat16)
            o_buf[h, pl.ds(c * (chunk // per_frame), chunk // per_frame)] = result.reshape(
                chunk // per_frame, per_frame, HD)
            return carry

        lax.fori_loop(0, tokens // chunk, rows_of, 0)

    def step_of(h, carry):
        @pl.when(h + ahead < heads)
        def _():
            send(h + ahead)

        if relay_refs:
            @pl.when(h + relay_ahead < heads)
            def _():
                forward(h + relay_ahead)

        @pl.when(has_left)
        def _():
            to_side(h, 0).wait_recv()

        @pl.when(has_right)
        def _():
            to_side(h, 1).wait_recv()

        attend(h)
        to_self(h).start()
        for step in range(1, head):
            to_part(h, step).start()
        return carry

    lax.fori_loop(0, heads, step_of, 0)

    def finish(h, carry):
        @pl.when(has_right)
        def _():
            to_side(h, 0).wait_send()

        @pl.when(has_left)
        def _():
            to_side(h, 1).wait_send()

        if relay_refs:
            for side in range(2):
                @pl.when(relays(h, side))
                def _():
                    from_relay(h, side).wait_send()

        to_self(h).wait()
        for step in range(1, head):
            to_part(h, step).wait_send()
            to_part(h, step).wait_recv()
        return carry

    lax.fori_loop(0, heads, finish, 0)


def on_device(queries, key_field, value_field):
    frames, height, width, feat = queries.shape
    seq = lax.axis_size("seq")
    head = lax.axis_size("head")
    heads = feat // HD
    tokens = frames * height * width
    rows = height // head * width
    relay_scratch = []
    if seq == 16 and head == 2:
        relay_scratch = [
            pltpu.VMEM((heads, 2, tokens, HD), jnp.bfloat16),
            pltpu.SemaphoreType.DMA((heads,)),
            pltpu.SemaphoreType.DMA((heads,)),
        ]
    result = pl.pallas_call(
        functools.partial(kernel, seq=seq, head=head),
        out_shape=pltpu.VMEM((frames, rows, feat * head), jnp.bfloat16),
        in_specs=[pl.BlockSpec(memory_space=pl.ANY)] * 3,
        out_specs=pl.BlockSpec(memory_space=pltpu.VMEM),
        scratch_shapes=[
            pltpu.VMEM((heads, tokens, HD), jnp.bfloat16),
            pltpu.VMEM((3, heads, 2, tokens, HD), jnp.bfloat16),
            pltpu.VMEM((heads, frames, height * width, HD), jnp.bfloat16),
            pltpu.SemaphoreType.DMA((3, heads)),
            pltpu.SemaphoreType.DMA((2, heads)),
            pltpu.SemaphoreType.DMA((2, heads)),
            pltpu.SemaphoreType.DMA((heads,)),
            pltpu.SemaphoreType.DMA((head, heads)),
            pltpu.SemaphoreType.DMA((head, heads)),
        ] + relay_scratch,
        compiler_params=pltpu.CompilerParams(
            collective_id=0, has_side_effects=True, vmem_limit_bytes=56 * 2 ** 20
        ),
        cost_estimate=pl.CostEstimate(
            flops=12 * heads * tokens * tokens * HD,
            bytes_accessed=8 * tokens * feat,
            transcendentals=3 * heads * tokens * tokens,
        ),
        name="tile_attention",
    )(
        queries.reshape(tokens, feat),
        key_field.reshape(tokens, feat),
        value_field.reshape(tokens, feat),
    )
    return result.reshape(frames, height // head, width, feat * head)


def solution(mesh):
    spec = P(None, None, "seq", "head")
    return jax.shard_map(
        on_device, mesh=mesh, in_specs=(spec, spec, spec),
        out_specs=P(None, "head", "seq", None), check_vma=False,
    )
```

```python
import functools

import jax
import jax.numpy as jnp
from jax import lax
from jax.experimental import pallas as pl
from jax.experimental.pallas import tpu as pltpu
from jax.sharding import PartitionSpec as P

HD = 128
AHEAD = 3
RELAY_AHEAD = 1
LAG = 3
MISSING = 1e30
LOG2E = 1.4426950408889634


def kernel(q_ref, k_ref, v_ref, out_ref, q_buf, kv_buf, o_buf,
           load_sem, send_sem, recv_sem, own_sem, osend_sem, orecv_sem, *relay_refs, seq, head):
    heads = q_buf.shape[0]
    tokens = q_buf.shape[1]
    frames = o_buf.shape[1]
    rows = out_ref.shape[1]
    me = lax.axis_index("seq")
    part = lax.axis_index("head")
    has_left = me > 0
    has_right = me < seq - 1
    layers = seq // 4
    layer = me // 4
    low = me % 4 == 0
    high = me % 4 == 3
    if relay_refs:
        relay_buf, relay_send, relay_recv = relay_refs

    def columns(j):
        return pl.ds(pl.multiple_of(j * HD, HD), HD)

    def loads(h):
        return (
            pltpu.make_async_copy(k_ref.at[:, columns(h)], kv_buf.at[1, h, 0], load_sem.at[0, h]),
            pltpu.make_async_copy(v_ref.at[:, columns(h)], kv_buf.at[1, h, 1], load_sem.at[1, h]),
            pltpu.make_async_copy(q_ref.at[:, columns(h)], q_buf.at[h], load_sem.at[2, h]),
        )

    def to_side(h, side):
        target = me + 1 if side == 0 else me - 1
        return pltpu.make_async_remote_copy(
            src_ref=kv_buf.at[1, h],
            dst_ref=kv_buf.at[0 if side == 0 else 2, h],
            send_sem=send_sem.at[side, h],
            recv_sem=recv_sem.at[side, h],
            device_id={"seq": target},
            device_id_type=pl.DeviceIdType.MESH,
        )

    def to_relay(h, side):
        return pltpu.make_async_remote_copy(
            src_ref=kv_buf.at[1, h],
            dst_ref=relay_buf.at[h],
            send_sem=send_sem.at[side, h],
            recv_sem=relay_recv.at[h],
            device_id={"seq": me - 2 if side == 0 else me + 2},
            device_id_type=pl.DeviceIdType.MESH,
        )

    def from_relay(h, side):
        return pltpu.make_async_remote_copy(
            src_ref=relay_buf.at[h],
            dst_ref=kv_buf.at[0 if side == 0 else 2, h],
            send_sem=relay_send.at[h],
            recv_sem=recv_sem.at[side, h],
            device_id={"seq": me + 3 if side == 0 else me - 3},
            device_id_type=pl.DeviceIdType.MESH,
        )

    def relayed(h, side, at):
        return h % layers < (layers - 1 - at if side == 0 else at)

    def relays(h, side):
        if side == 0:
            return (me % 4 == 1) & (layer < layers - 1) & relayed(h, 0, layer)
        return (me % 4 == 2) & (layer > 0) & relayed(h, 1, layer)

    def forward(h):
        for side in range(2):
            @pl.when(relays(h, side))
            def _():
                to_relay(h, side).wait_recv()
                from_relay(h, side).start()

    def out_slices(h, p, sender):
        src = o_buf.at[h, :, pl.ds(pl.multiple_of(p * rows, 16), rows), :]
        dst = out_ref.at[:, :, columns(sender * heads + h)]
        return src, dst

    def to_part(h, step):
        p = lax.rem(part + step, head)
        src, dst = out_slices(h, p, part)
        return pltpu.make_async_remote_copy(
            src_ref=src,
            dst_ref=dst,
            send_sem=osend_sem.at[step, h],
            recv_sem=orecv_sem.at[step, h],
            device_id={"head": p},
            device_id_type=pl.DeviceIdType.MESH,
        )

    def to_self(h):
        src, dst = out_slices(h, part, part)
        return pltpu.make_async_copy(src, dst, own_sem.at[h])

    def start_loads(h, carry):
        for copy in loads(h):
            copy.start()
        return carry

    lax.fori_loop(0, heads, start_loads, 0)

    barrier = pltpu.get_barrier_semaphore()
    offsets = (1, seq - 1) + ((2, 3, seq - 2, seq - 3) if relay_refs else ())
    for offset in offsets:
        near = lax.rem(me + offset, seq)
        pl.semaphore_signal(barrier, inc=1, device_id={"seq": near}, device_id_type=pl.DeviceIdType.MESH)
    for step in range(1, head):
        pl.semaphore_signal(barrier, inc=1, device_id={"head": lax.rem(part + step, head)},
                            device_id_type=pl.DeviceIdType.MESH)
    pl.semaphore_wait(barrier, len(offsets) + head - 1)

    def send(h):
        for copy in loads(h):
            copy.wait()

        for side, exists, edge in ((0, has_right, high), (1, has_left, low)):
            if relay_refs:
                by_relay = edge & relayed(h, side, layer)

                @pl.when(exists & by_relay)
                def _():
                    to_relay(h, side).start()

                exists = exists & jnp.logical_not(by_relay)

            @pl.when(exists)
            def _():
                to_side(h, side).start()

    ahead = min(AHEAD, heads)

    def first_sends(h, carry):
        send(h)
        return carry

    lax.fori_loop(0, ahead, first_sends, 0)

    @pl.when(jnp.logical_not(has_left))
    def _():
        kv_buf[0] = jnp.zeros_like(kv_buf[0])

    @pl.when(jnp.logical_not(has_right))
    def _():
        kv_buf[2] = jnp.zeros_like(kv_buf[2])

    shift = (
        jnp.where(has_left, 0.0, MISSING).astype(jnp.float32),
        jnp.float32(0.0),
        jnp.where(has_right, 0.0, MISSING).astype(jnp.float32),
    )
    chunk = 256 if tokens % 256 == 0 else tokens
    factor = HD ** -0.5 * LOG2E
    per_frame = tokens // frames

    relay_ahead = min(RELAY_AHEAD, heads)
    if relay_refs:
        def first_forwards(h, carry):
            forward(h)
            return carry

        lax.fori_loop(0, relay_ahead, first_forwards, 0)

    def attend(h):
        def rows_of(c, carry):
            at = pl.ds(pl.multiple_of(c * chunk, chunk), chunk)
            q = q_buf[h, at, :]
            scores = [
                lax.dot_general(q, kv_buf[b, h, 0], (((1,), (1,)), ((), ())),
                                preferred_element_type=jnp.float32)
                for b in range(3)
            ]
            tops = [jnp.max(s, axis=1, keepdims=True) - shift[b] for b, s in enumerate(scores)]
            top = jnp.maximum(jnp.maximum(tops[0], tops[1]), tops[2])
            total = 0.0
            weight_sum = 0.0
            for b in range(3):
                w = jnp.exp2(scores[b] * factor - (top + shift[b]) * factor)
                weight_sum = weight_sum + jnp.sum(w, axis=1, keepdims=True)
                total = total + jnp.dot(w.astype(jnp.bfloat16), kv_buf[b, h, 1],
                                        preferred_element_type=jnp.float32)
            result = (total / weight_sum).astype(jnp.bfloat16)
            o_buf[h, pl.ds(c * (chunk // per_frame), chunk // per_frame)] = result.reshape(
                chunk // per_frame, per_frame, HD)
            return carry

        lax.fori_loop(0, tokens // chunk, rows_of, 0, unroll=True)

    lag = min(LAG, heads)

    def finish(h, carry):
        @pl.when(has_right)
        def _():
            to_side(h, 0).wait_send()

        @pl.when(has_left)
        def _():
            to_side(h, 1).wait_send()

        if relay_refs:
            for side in range(2):
                @pl.when(relays(h, side))
                def _():
                    from_relay(h, side).wait_send()

        to_self(h).wait()
        for step in range(1, head):
            to_part(h, step).wait_send()
            to_part(h, step).wait_recv()
        return carry

    def step_of(h, carry):
        @pl.when(h >= lag)
        def _():
            finish(h - lag, 0)

        @pl.when(h + ahead < heads)
        def _():
            send(h + ahead)

        if relay_refs:
            @pl.when(h + relay_ahead < heads)
            def _():
                forward(h + relay_ahead)

        @pl.when(has_left)
        def _():
            to_side(h, 0).wait_recv()

        @pl.when(has_right)
        def _():
            to_side(h, 1).wait_recv()

        attend(h)
        to_self(h).start()
        for step in range(1, head):
            to_part(h, step).start()
        return carry

    lax.fori_loop(0, heads, step_of, 0)

    lax.fori_loop(heads - lag, heads, finish, 0)


def on_device(queries, key_field, value_field):
    frames, height, width, feat = queries.shape
    seq = lax.axis_size("seq")
    head = lax.axis_size("head")
    heads = feat // HD
    tokens = frames * height * width
    rows = height // head * width
    relay_scratch = []
    if seq == 16 and head == 2:
        relay_scratch = [
            pltpu.VMEM((heads, 2, tokens, HD), jnp.bfloat16),
            pltpu.SemaphoreType.DMA((heads,)),
            pltpu.SemaphoreType.DMA((heads,)),
        ]
    result = pl.pallas_call(
        functools.partial(kernel, seq=seq, head=head),
        out_shape=pltpu.VMEM((frames, rows, feat * head), jnp.bfloat16),
        in_specs=[pl.BlockSpec(memory_space=pl.ANY)] * 3,
        out_specs=pl.BlockSpec(memory_space=pltpu.VMEM),
        scratch_shapes=[
            pltpu.VMEM((heads, tokens, HD), jnp.bfloat16),
            pltpu.VMEM((3, heads, 2, tokens, HD), jnp.bfloat16),
            pltpu.VMEM((heads, frames, height * width, HD), jnp.bfloat16),
            pltpu.SemaphoreType.DMA((3, heads)),
            pltpu.SemaphoreType.DMA((2, heads)),
            pltpu.SemaphoreType.DMA((2, heads)),
            pltpu.SemaphoreType.DMA((heads,)),
            pltpu.SemaphoreType.DMA((head, heads)),
            pltpu.SemaphoreType.DMA((head, heads)),
        ] + relay_scratch,
        compiler_params=pltpu.CompilerParams(
            collective_id=0, has_side_effects=True, vmem_limit_bytes=56 * 2 ** 20
        ),
        cost_estimate=pl.CostEstimate(
            flops=12 * heads * tokens * tokens * HD,
            bytes_accessed=8 * tokens * feat,
            transcendentals=3 * heads * tokens * tokens,
        ),
        name="tile_attention",
    )(
        queries.reshape(tokens, feat),
        key_field.reshape(tokens, feat),
        value_field.reshape(tokens, feat),
    )
    return result.reshape(frames, height // head, width, feat * head)


def solution(mesh):
    spec = P(None, None, "seq", "head")
    return jax.shard_map(
        on_device, mesh=mesh, in_specs=(spec, spec, spec),
        out_specs=P(None, "head", "seq", None), check_vma=False,
    )
```

```python
import functools

import jax
import jax.numpy as jnp
from jax import lax
from jax.experimental import pallas as pl
from jax.experimental.pallas import tpu as pltpu
from jax.sharding import PartitionSpec as P

HD = 128
AHEAD = 3
RELAY_AHEAD = 1
LAG = 3
MISSING = 1e30
LOG2E = 1.4426950408889634


def kernel(q_ref, k_ref, v_ref, out_ref, q_buf, kv_buf, o_buf,
           load_sem, send_sem, recv_sem, own_sem, osend_sem, orecv_sem, *relay_refs, seq, head):
    heads = q_buf.shape[0]
    tokens = q_buf.shape[1]
    frames = o_buf.shape[1]
    rows = out_ref.shape[1]
    me = lax.axis_index("seq")
    part = lax.axis_index("head")
    has_left = me > 0
    has_right = me < seq - 1
    layers = seq // 4
    layer = me // 4
    low = me % 4 == 0
    high = me % 4 == 3
    if relay_refs:
        relay_buf, relay_send, relay_recv = relay_refs

    def columns(j):
        return pl.ds(pl.multiple_of(j * HD, HD), HD)

    def loads(h):
        return (
            pltpu.make_async_copy(k_ref.at[:, columns(h)], kv_buf.at[1, h, 0], load_sem.at[0, h]),
            pltpu.make_async_copy(v_ref.at[:, columns(h)], kv_buf.at[1, h, 1], load_sem.at[1, h]),
            pltpu.make_async_copy(q_ref.at[:, columns(h)], q_buf.at[h], load_sem.at[2, h]),
        )

    def to_side(h, side):
        target = me + 1 if side == 0 else me - 1
        return pltpu.make_async_remote_copy(
            src_ref=kv_buf.at[1, h],
            dst_ref=kv_buf.at[0 if side == 0 else 2, h],
            send_sem=send_sem.at[side, h],
            recv_sem=recv_sem.at[side, h],
            device_id={"seq": target},
            device_id_type=pl.DeviceIdType.MESH,
        )

    def to_relay(h, side):
        return pltpu.make_async_remote_copy(
            src_ref=kv_buf.at[1, h],
            dst_ref=relay_buf.at[h],
            send_sem=send_sem.at[side, h],
            recv_sem=relay_recv.at[h],
            device_id={"seq": me - 2 if side == 0 else me + 2},
            device_id_type=pl.DeviceIdType.MESH,
        )

    def from_relay(h, side):
        return pltpu.make_async_remote_copy(
            src_ref=relay_buf.at[h],
            dst_ref=kv_buf.at[0 if side == 0 else 2, h],
            send_sem=relay_send.at[h],
            recv_sem=recv_sem.at[side, h],
            device_id={"seq": me + 3 if side == 0 else me - 3},
            device_id_type=pl.DeviceIdType.MESH,
        )

    def relayed(h, side, at):
        return h % layers < (layers - 1 - at if side == 0 else at)

    def relays(h, side):
        if side == 0:
            return (me % 4 == 1) & (layer < layers - 1) & relayed(h, 0, layer)
        return (me % 4 == 2) & (layer > 0) & relayed(h, 1, layer)

    def forward(h):
        for side in range(2):
            @pl.when(relays(h, side))
            def _():
                to_relay(h, side).wait_recv()
                from_relay(h, side).start()

    def out_slices(h, p, sender):
        src = o_buf.at[h, :, pl.ds(pl.multiple_of(p * rows, 16), rows), :]
        dst = out_ref.at[:, :, columns(sender * heads + h)]
        return src, dst

    def to_part(h, step):
        p = lax.rem(part + step, head)
        src, dst = out_slices(h, p, part)
        return pltpu.make_async_remote_copy(
            src_ref=src,
            dst_ref=dst,
            send_sem=osend_sem.at[step, h],
            recv_sem=orecv_sem.at[step, h],
            device_id={"head": p},
            device_id_type=pl.DeviceIdType.MESH,
        )

    def to_self(h):
        src, dst = out_slices(h, part, part)
        return pltpu.make_async_copy(src, dst, own_sem.at[h])

    def start_loads(h, carry):
        for copy in loads(h):
            copy.start()
        return carry

    lax.fori_loop(0, heads, start_loads, 0)

    barrier = pltpu.get_barrier_semaphore()
    offsets = (1, seq - 1) + ((2, 3, seq - 2, seq - 3) if relay_refs else ())
    for offset in offsets:
        near = lax.rem(me + offset, seq)
        pl.semaphore_signal(barrier, inc=1, device_id={"seq": near}, device_id_type=pl.DeviceIdType.MESH)
    for step in range(1, head):
        pl.semaphore_signal(barrier, inc=1, device_id={"head": lax.rem(part + step, head)},
                            device_id_type=pl.DeviceIdType.MESH)
    pl.semaphore_wait(barrier, len(offsets) + head - 1)

    def send(h):
        for copy in loads(h):
            copy.wait()

        for side, exists, edge in ((0, has_right, high), (1, has_left, low)):
            if relay_refs:
                by_relay = edge & relayed(h, side, layer)

                @pl.when(exists & by_relay)
                def _():
                    to_relay(h, side).start()

                exists = exists & jnp.logical_not(by_relay)

            @pl.when(exists)
            def _():
                to_side(h, side).start()

    ahead = min(AHEAD, heads)

    def first_sends(h, carry):
        send(h)
        return carry

    lax.fori_loop(0, ahead, first_sends, 0)

    @pl.when(jnp.logical_not(has_left))
    def _():
        kv_buf[0] = jnp.zeros_like(kv_buf[0])

    @pl.when(jnp.logical_not(has_right))
    def _():
        kv_buf[2] = jnp.zeros_like(kv_buf[2])

    shift = (
        jnp.where(has_left, 0.0, MISSING).astype(jnp.float32),
        jnp.float32(0.0),
        jnp.where(has_right, 0.0, MISSING).astype(jnp.float32),
    )
    chunk = 256 if tokens % 256 == 0 else tokens
    factor = HD ** -0.5 * LOG2E
    per_frame = tokens // frames

    relay_ahead = min(RELAY_AHEAD, heads)
    if relay_refs:
        def first_forwards(h, carry):
            forward(h)
            return carry

        lax.fori_loop(0, relay_ahead, first_forwards, 0)

    def attend(h):
        def rows_of(c, carry):
            at = pl.ds(pl.multiple_of(c * chunk, chunk), chunk)
            q = q_buf[h, at, :]
            scores = [
                lax.dot_general(q, kv_buf[b, h, 0], (((1,), (1,)), ((), ())),
                                preferred_element_type=jnp.float32)
                for b in range(3)
            ]
            tops = [jnp.max(s, axis=1, keepdims=True) - shift[b] for b, s in enumerate(scores)]
            top = jnp.maximum(jnp.maximum(tops[0], tops[1]), tops[2])
            total = 0.0
            ones = jnp.ones((tokens, HD), jnp.bfloat16)
            for b in range(3):
                w = jnp.exp2(scores[b] * factor - (top + shift[b]) * factor)
                values = jnp.concatenate([kv_buf[b, h, 1], ones], axis=1)
                total = total + jnp.dot(w.astype(jnp.bfloat16), values,
                                        preferred_element_type=jnp.float32)
            result = (total[:, :HD] / total[:, HD:]).astype(jnp.bfloat16)
            o_buf[h, pl.ds(c * (chunk // per_frame), chunk // per_frame)] = result.reshape(
                chunk // per_frame, per_frame, HD)
            return carry

        lax.fori_loop(0, tokens // chunk, rows_of, 0, unroll=True)

    lag = min(LAG, heads)

    def finish(h, carry):
        @pl.when(has_right)
        def _():
            to_side(h, 0).wait_send()

        @pl.when(has_left)
        def _():
            to_side(h, 1).wait_send()

        if relay_refs:
            for side in range(2):
                @pl.when(relays(h, side))
                def _():
                    from_relay(h, side).wait_send()

        to_self(h).wait()
        for step in range(1, head):
            to_part(h, step).wait_send()
            to_part(h, step).wait_recv()
        return carry

    def step_of(h, carry):
        @pl.when(h >= lag)
        def _():
            finish(h - lag, 0)

        @pl.when(h + ahead < heads)
        def _():
            send(h + ahead)

        if relay_refs:
            @pl.when(h + relay_ahead < heads)
            def _():
                forward(h + relay_ahead)

        @pl.when(has_left)
        def _():
            to_side(h, 0).wait_recv()

        @pl.when(has_right)
        def _():
            to_side(h, 1).wait_recv()

        attend(h)
        to_self(h).start()
        for step in range(1, head):
            to_part(h, step).start()
        return carry

    lax.fori_loop(0, heads, step_of, 0)

    lax.fori_loop(heads - lag, heads, finish, 0)


def on_device(queries, key_field, value_field):
    frames, height, width, feat = queries.shape
    seq = lax.axis_size("seq")
    head = lax.axis_size("head")
    heads = feat // HD
    tokens = frames * height * width
    rows = height // head * width
    relay_scratch = []
    if seq == 16 and head == 2:
        relay_scratch = [
            pltpu.VMEM((heads, 2, tokens, HD), jnp.bfloat16),
            pltpu.SemaphoreType.DMA((heads,)),
            pltpu.SemaphoreType.DMA((heads,)),
        ]
    result = pl.pallas_call(
        functools.partial(kernel, seq=seq, head=head),
        out_shape=pltpu.VMEM((frames, rows, feat * head), jnp.bfloat16),
        in_specs=[pl.BlockSpec(memory_space=pl.ANY)] * 3,
        out_specs=pl.BlockSpec(memory_space=pltpu.VMEM),
        scratch_shapes=[
            pltpu.VMEM((heads, tokens, HD), jnp.bfloat16),
            pltpu.VMEM((3, heads, 2, tokens, HD), jnp.bfloat16),
            pltpu.VMEM((heads, frames, height * width, HD), jnp.bfloat16),
            pltpu.SemaphoreType.DMA((3, heads)),
            pltpu.SemaphoreType.DMA((2, heads)),
            pltpu.SemaphoreType.DMA((2, heads)),
            pltpu.SemaphoreType.DMA((heads,)),
            pltpu.SemaphoreType.DMA((head, heads)),
            pltpu.SemaphoreType.DMA((head, heads)),
        ] + relay_scratch,
        compiler_params=pltpu.CompilerParams(
            collective_id=0, has_side_effects=True, vmem_limit_bytes=56 * 2 ** 20
        ),
        cost_estimate=pl.CostEstimate(
            flops=12 * heads * tokens * tokens * HD,
            bytes_accessed=8 * tokens * feat,
            transcendentals=3 * heads * tokens * tokens,
        ),
        name="tile_attention",
    )(
        queries.reshape(tokens, feat),
        key_field.reshape(tokens, feat),
        value_field.reshape(tokens, feat),
    )
    return result.reshape(frames, height // head, width, feat * head)


def solution(mesh):
    spec = P(None, None, "seq", "head")
    return jax.shard_map(
        on_device, mesh=mesh, in_specs=(spec, spec, spec),
        out_specs=P(None, "head", "seq", None), check_vma=False,
    )
```
